32 devices in a mesh: group: 2 (over x), tp: 16 (over z, y, core), pool: 1.
Axes of the slice: x: 2, y: 2, z: 4, core: 2. Of those that a mesh axis runs over, the one named last changes fastest.
Arguments:
- prompt_x: bfloat16 [2048, 8192], P(('group', 'pool'), 'tp'), parts along dimension 0, may hold values from -6 to 6
- decode_x: bfloat16 [4, 32, 8192], P(None, ('group', 'pool'), 'tp'), parts along dimension 1, may hold values from -240 to 240
- w_query: bfloat16 [8192, 8192], P(None, 'tp'), may hold values from -0.0625 to 0.0625
- w_keyval: bfloat16 [8192, 2048], P('tp'), may hold values from -0.0625 to 0.0625
- w_out: bfloat16 [8192, 8192], P('tp'), may hold values from -0.0625 to 0.0625
- prompt_blocks: int32 [32], P('group'), parts along dimension 0, may hold values from 1 to 32, 64 in all
- prompt_row: int32 [32], P('group'), parts along dimension 0, may hold values from 0 to 15, each once
Outputs:
- decode_out: bfloat16 [4, 32, 8192], P(None, ('group', 'pool'), 'tp'), parts along dimension 1
The draws below stay inside these ranges and needn't reach their ends.
There are 2 independent parts, one for each index of `group`. The reference program is written for one: setup_inputs(seed, part) draws one part's arguments, and reference() takes and returns one part's arrays. A program takes and returns all parts, laid end to end along the dimension named above; an argument that names none is the same for every part. Nothing has to cross between parts.
Inputs may be any that keep to these rules, and one draw needn't show every extreme that they name: `prompt_blocks`: each prompt has at least one block, the prompts fill the span exactly, and one prompt has exactly 32 blocks. `prompt_row`: every decode row continues exactly one prompt.
All inputs are finite; a program needn't handle non-finite values. Where the reference program divides by a largest or mean magnitude, that divisor is 1e-20 or more.
Results may differ from the reference program's by a relative error of at most 0.018.
Values may be sent and summed in bfloat16 or wider, within the bound.
A program may use at most 128 MiB of HBM per device.

```python
import math
import jax
import jax.numpy as jnp
import numpy as np
from jax import lax

D = 8192
HQ = 64
KVH = 8
HD = 128
BLK = 16
STEPS = 4
MOSTB = 32
PRE_TOK = 1024
NBLK = 64
ROWS = 16


def draw_decode_x(key, part):
    base = jnp.clip(jax.random.normal(key, (STEPS, ROWS, D), jnp.float32), -6.0, 6.0)
    return base.astype(jnp.bfloat16)


def steps_of(rng, dims, split, smallest, largest):
    def one(dim, blocks):
        heights = jax.random.uniform(jax.random.fold_in(jax.random.fold_in(rng, 6), dim), (blocks,), jnp.float32, smallest / len(split), largest / len(split))
        return jnp.repeat(jnp.exp(heights), dims[dim] // blocks).reshape((-1,) + (1,) * (len(dims) - dim - 1))

    factor_of = one(*split[0])
    for cut in split[1:]:
        factor_of = factor_of * one(*cut)
    return factor_of


def length_profile(amount, total, reach, slope):
    weights = [(1 << 20) // math.isqrt(grade ** slope) + 1 for grade in range(2, amount + 1)]
    surplus, counts = total - reach - (amount - 1), [1] * (amount - 1)
    while surplus > 0:
        free = [i for i in range(amount - 1) if counts[i] < reach]
        pool, left = sum([weights[i] for i in free]), surplus
        for i in free:
            addition = min(reach - counts[i], max(1, left * weights[i] // pool), surplus)
            counts[i] = counts[i] + addition
            surplus = surplus - addition
    return np.array([reach] + counts)


def ragged_sizes(stream_key, count, total, most, lean):
    if count == 2:
        one = jax.random.randint(stream_key, (), max(1, total - most), min(most, total - 1) + 1)
        return jnp.stack([one, total - one])
    lengths = jnp.asarray(length_profile(count, total, most, lean), jnp.int32)
    twos = (count - 1) // 2
    source_of, taker = lengths[1:1 + 2 * twos:2], lengths[2:2 + 2 * twos:2]
    slack = jnp.minimum(source_of - 1, most - taker)
    shifted = jax.random.randint(jax.random.fold_in(stream_key, 1), (twos,), 0, 1 << 20) % (slack + 1)
    lengths = lengths.at[1:1 + 2 * twos:2].set(source_of - shifted).at[2:2 + 2 * twos:2].set(taker + shifted)
    return lengths[jax.random.permutation(jax.random.fold_in(stream_key, 2), count)]


def normal_values(rng, shape, spread, reach, pieces=(), held_as=jnp.bfloat16):
    array = spread * jax.random.normal(rng, shape, jnp.float32)
    if pieces:
        array = array * steps_of(rng, shape, pieces, -0.22, 0.18)
    return jnp.clip(array, -reach, reach).astype(held_as)


def setup_inputs(seed: int = 0, part: int = 0) -> dict:
    seeds = jax.random.split(jax.random.key(seed), 8)
    own_keys = jax.random.split(jax.random.fold_in(seeds[7], part), 8)
    prompt_x = normal_values(own_keys[0], (PRE_TOK, D), 1.0, 6.0, ((1, 16),))
    decode_x = draw_decode_x(jax.random.fold_in(jax.random.fold_in(seeds[7], part), 71), part)
    w_query = normal_values(seeds[2], (D, HQ * HD), D ** -0.5, 0.0625, ((1, 16),))
    w_keyval = normal_values(seeds[3], (D, KVH * 2 * HD), D ** -0.5, 0.0625, ((0, 16),))
    w_out = normal_values(seeds[4], (HQ * HD, D), (HQ * HD) ** -0.5, 0.0625, ((0, 16),))
    prompt_blocks = ragged_sizes(own_keys[5], ROWS, NBLK, MOSTB, 2).astype(jnp.int32)
    prompt_row = jax.random.permutation(own_keys[6], ROWS).astype(jnp.int32)
    return dict(prompt_x=prompt_x, decode_x=decode_x, w_query=w_query, w_keyval=w_keyval, w_out=w_out, prompt_blocks=prompt_blocks, prompt_row=prompt_row)


def block_rows(prompt_blocks, prompt_row, total_blocks):
    block_ends = jnp.cumsum(prompt_blocks).astype(jnp.int32)
    positions = jnp.arange(total_blocks, dtype=jnp.int32)
    owner_seq = lax.optimization_barrier(jnp.sum((block_ends[None, :] <= positions[:, None]).astype(jnp.int32), axis=1))
    seq_match = owner_seq[:, None] == jnp.arange(prompt_row.shape[0], dtype=jnp.int32)[None, :]
    return lax.optimization_barrier(jnp.sum(jnp.where(seq_match, prompt_row[None, :], 0), axis=1)).astype(jnp.int32)

def attend(queries, cache_vals, cache_scale, slot_row, fresh_keyval, row_ids):
    head_dim = queries.shape[-1]
    inverse_root = 1.0 / math.sqrt(head_dim)
    query_f32 = queries.astype(jnp.float32)
    scale_f32 = cache_scale.astype(jnp.float32)
    cache_keys = cache_vals[:, :, :head_dim].astype(jnp.float32) * scale_f32[:, 0][:, None, None]
    cache_values = cache_vals[:, :, head_dim:].astype(jnp.float32) * scale_f32[:, 1][:, None, None]
    cache_score = jnp.einsum('srgd,nkd->srgnk', query_f32, cache_keys) * inverse_root
    visible = slot_row[None, :] == row_ids[:, None]
    cache_score = jnp.where(visible[None, :, None, :, None], cache_score, -jnp.inf)
    fresh_f32 = fresh_keyval.astype(jnp.float32)
    fresh_score = jnp.einsum('srgd,trd->srgt', query_f32, fresh_f32[:, :, :head_dim]) * inverse_root
    step_index = jnp.arange(queries.shape[0], dtype=jnp.int32)
    causal = step_index[:, None] >= step_index[None, :]
    fresh_score = jnp.where(causal[:, None, None, :], fresh_score, -jnp.inf)
    top_score = jnp.maximum(lax.optimization_barrier(jnp.max(cache_score, axis=(3, 4))), lax.optimization_barrier(jnp.max(fresh_score, axis=3)))
    cache_weight = jnp.exp(cache_score - top_score[..., None, None])
    fresh_weight = jnp.exp(fresh_score - top_score[..., None])
    denominator = lax.optimization_barrier(jnp.sum(cache_weight, axis=(3, 4))) + lax.optimization_barrier(jnp.sum(fresh_weight, axis=3))
    weighted = jnp.einsum('srgnk,nkd->srgd', cache_weight, cache_values)
    weighted = weighted + jnp.einsum('srgt,trd->srgd', fresh_weight, fresh_f32[:, :, head_dim:])
    return weighted / denominator[..., None]

def reference(prompt_x, decode_x, w_query, w_keyval, w_out, prompt_blocks, prompt_row):
    keyval = jnp.dot(prompt_x, w_keyval, preferred_element_type=jnp.float32)
    total_blocks = keyval.shape[0] // BLK
    blocked = keyval.reshape(total_blocks, BLK, KVH, 2, HD)
    scales = (lax.optimization_barrier(jnp.max(jnp.abs(blocked), axis=(1, 4))) + 1e-06).astype(jnp.bfloat16)
    stored = (blocked / scales.astype(jnp.float32)[:, None, :, :, None]).astype(jnp.bfloat16)
    stored = stored.reshape(total_blocks, BLK, KVH, 2 * HD).transpose(2, 0, 1, 3)
    scales = scales.transpose(1, 0, 2)
    slot_row = block_rows(prompt_blocks, prompt_row, total_blocks)
    step_count, row_count, model_width = decode_x.shape
    flat_rows = decode_x.reshape(step_count * row_count, model_width)
    queries = jnp.dot(flat_rows, w_query, preferred_element_type=jnp.float32).astype(jnp.bfloat16)
    queries = queries.reshape(step_count, row_count, KVH, HQ // KVH, HD).transpose(2, 0, 1, 3, 4)
    fresh_keyval = jnp.dot(flat_rows, w_keyval, preferred_element_type=jnp.float32).astype(jnp.bfloat16)
    fresh_keyval = fresh_keyval.reshape(step_count, row_count, KVH, 2 * HD).transpose(2, 0, 1, 3)
    row_ids = jnp.arange(row_count, dtype=jnp.int32)

    def per_head(head_inputs):
        return attend(head_inputs[0], head_inputs[1], head_inputs[2], slot_row, head_inputs[3], row_ids)
    weighted = lax.map(per_head, (queries, stored, scales, fresh_keyval))
    attended = weighted.transpose(1, 2, 0, 3, 4).reshape(step_count * row_count, HQ * HD).astype(jnp.bfloat16)
    decode_out = jnp.dot(attended, w_out, preferred_element_type=jnp.float32).astype(jnp.bfloat16)
    return decode_out.reshape(step_count, row_count, model_width)
```

```python
import functools
import math

import jax
import jax.numpy as jnp
import numpy as np
from jax import lax
from jax.experimental import pallas as pl
from jax.experimental.pallas import tpu as pltpu
from jax.sharding import PartitionSpec as P

KVH = 8
HD = 128
BLK = 16


def block_rows(prompt_blocks, prompt_row, total_blocks):
    order = jnp.arange(prompt_blocks.shape[0], dtype=jnp.int32)
    block_ends = jnp.sum(jnp.where(order[None, :] <= order[:, None], prompt_blocks[None, :], 0), axis=1)
    positions = jnp.arange(total_blocks, dtype=jnp.int32)
    owner_seq = jnp.sum((block_ends[None, :] <= positions[:, None]).astype(jnp.int32), axis=1)
    seq_match = owner_seq[:, None] == jnp.arange(prompt_row.shape[0], dtype=jnp.int32)[None, :]
    return jnp.sum(jnp.where(seq_match, prompt_row[None, :], 0), axis=1)


def attend(queries, cache_vals, cache_scale, slot_row, fresh_keyval, row_ids):
    head_dim = queries.shape[-1]
    inverse_root = 1.0 / math.sqrt(head_dim)
    query_f32 = queries.astype(jnp.float32)
    scale_f32 = cache_scale.astype(jnp.float32)
    cache_keys = cache_vals[:, :, :head_dim].astype(jnp.float32) * scale_f32[:, 0][:, None, None]
    cache_values = cache_vals[:, :, head_dim:].astype(jnp.float32) * scale_f32[:, 1][:, None, None]
    cache_score = jnp.einsum("srgd,nkd->srgnk", query_f32, cache_keys) * inverse_root
    visible = slot_row[None, :] == row_ids[:, None]
    cache_score = jnp.where(visible[None, :, None, :, None], cache_score, -jnp.inf)
    fresh_f32 = fresh_keyval.astype(jnp.float32)
    fresh_score = jnp.einsum("srgd,trd->srgt", query_f32, fresh_f32[:, :, :head_dim]) * inverse_root
    step_index = jnp.arange(queries.shape[0], dtype=jnp.int32)
    causal = step_index[:, None] >= step_index[None, :]
    fresh_score = jnp.where(causal[:, None, None, :], fresh_score, -jnp.inf)
    top_score = jnp.maximum(jnp.max(cache_score, axis=(3, 4)), jnp.max(fresh_score, axis=3))
    cache_weight = jnp.exp(cache_score - top_score[..., None, None])
    fresh_weight = jnp.exp(fresh_score - top_score[..., None])
    denominator = jnp.sum(cache_weight, axis=(3, 4)) + jnp.sum(fresh_weight, axis=3)
    weighted = jnp.einsum("srgnk,nkd->srgd", cache_weight, cache_values)
    weighted = weighted + jnp.einsum("srgt,trd->srgd", fresh_weight, fresh_f32[:, :, head_dim:])
    return weighted / denominator[..., None]


def on_device(prompt_x, decode_x, w_query, w_keyval, w_out, prompt_blocks, prompt_row):
    tp_count = lax.axis_size("tp")
    pool_count = lax.axis_size("pool")
    tp_index = lax.axis_index("tp")
    pool_index = lax.axis_index("pool")
    half_tokens = prompt_x.shape[0]
    tokens_here = half_tokens // tp_count
    blocks_here = tokens_here // BLK
    half_blocks = half_tokens // BLK
    total_blocks = half_blocks * pool_count
    keyval = lax.psum_scatter(
        jnp.dot(prompt_x, w_keyval, preferred_element_type=jnp.float32),
        "tp",
        scatter_dimension=0,
        tiled=True,
    )
    blocked = keyval.reshape(blocks_here, BLK, KVH, 2, HD)
    scales = (jnp.max(jnp.abs(blocked), axis=(1, 4)) + 1e-06).astype(jnp.bfloat16)
    stored = (blocked / scales.astype(jnp.float32)[:, None, :, :, None]).astype(jnp.bfloat16)
    stored = stored.reshape(blocks_here, BLK, KVH, 2 * HD)
    slot_row_all = block_rows(prompt_blocks, prompt_row, total_blocks)
    row_half = decode_x.shape[1]
    owner_half = slot_row_all // row_half
    first_block = pool_index * half_blocks + tp_index * blocks_here
    mine_owner = lax.dynamic_slice_in_dim(owner_half, first_block, blocks_here, 0)
    dest_head = np.arange(tp_count) * KVH // tp_count
    by_head = jnp.stack([stored[:, :, int(h)] for h in dest_head])
    scale_head = jnp.stack([scales[:, int(h)] for h in dest_head])
    to_half = mine_owner[None, :] == jnp.arange(pool_count, dtype=jnp.int32)[:, None]
    zero_value = jnp.zeros((), jnp.bfloat16)
    send_vals = jnp.where(to_half[None, :, :, None, None], by_head[:, None], zero_value)
    send_scale = jnp.where(to_half[None, :, :, None], scale_head[:, None], zero_value)
    got_vals, got_scale = (
        lax.all_to_all(
            lax.all_to_all(send_vals, "tp", split_axis=0, concat_axis=0, tiled=True),
            "pool",
            split_axis=1,
            concat_axis=1,
            tiled=True,
        ),
        lax.all_to_all(
            lax.all_to_all(send_scale, "tp", split_axis=0, concat_axis=0, tiled=True),
            "pool",
            split_axis=1,
            concat_axis=1,
            tiled=True,
        ),
    )
    got_vals = got_vals.reshape(total_blocks, BLK, 2 * HD)
    got_scale = got_scale.reshape(total_blocks, 2)
    slot_row = (
        slot_row_all.reshape(pool_count, tp_count, blocks_here)
        .transpose(1, 0, 2)
        .reshape(total_blocks)
    )
    gathered = lax.all_gather(decode_x, "tp", axis=2, tiled=True)
    step_count, row_count, model_width = gathered.shape
    heads_here = w_query.shape[1] // HD
    queries = jnp.einsum("srd,de->sre", gathered, w_query, preferred_element_type=jnp.float32)
    queries = queries.astype(jnp.bfloat16).reshape(step_count, row_count, heads_here, HD)
    partial_new = jnp.einsum("srd,de->sre", decode_x, w_keyval, preferred_element_type=jnp.float32)
    summed_new = lax.psum(partial_new, "tp")
    fresh_keyval = summed_new.astype(jnp.bfloat16).reshape(step_count, row_count, KVH, 2 * HD)
    my_head = tp_index * KVH // tp_count
    fresh_keyval = lax.dynamic_index_in_dim(fresh_keyval, my_head, 2, keepdims=False)
    row_ids = pool_index * row_count + jnp.arange(row_count, dtype=jnp.int32)
    weighted = attend(queries, got_vals, got_scale, slot_row, fresh_keyval, row_ids)
    attended = weighted.reshape(step_count, row_count, heads_here * HD).astype(jnp.bfloat16)
    out_term = jnp.einsum("sre,ed->srd", attended, w_out, preferred_element_type=jnp.float32)
    return lax.psum_scatter(out_term, "tp", scatter_dimension=2, tiled=True).astype(jnp.bfloat16)


def fused(
    depth, rows,
    pb_ref, pr_ref, px_ref, dx_ref, wkv_ref, wq_ref, wo_ref,
    out_ref,
    xs, wk, wq, wo, dall,
    a_send, a_recv, a_own,
    b_send, b_recv,
    c_send, c_recv,
    kv,
    oa_send, oa_recv, oa_own,
    ob_send, ob_recv,
    oc_send, oc_recv,
    x_sem, wk_sem, wq_sem, wo_sem,
    g_sem, a_sem, b_sem, c_sem, kv_sem, oa_sem, ob_sem, oc_sem,
):
    me = lax.axis_index("tp")
    z, y, c = me // 4, lax.rem(me // 2, 2), lax.rem(me, 2)
    tokens, decodes = px_ref.shape[0], dx_ref.shape[0]
    feats = px_ref.shape[1]
    half = xs.shape[1]
    width = 2 * HD
    outw = out_ref.shape[1]
    order = list(range(1, depth)) + [0]

    def along(d):
        return lax.rem(z + d, depth)

    def index(zz, yy, cc):
        return (zz * 2 + yy) * 2 + cc

    core_peer = index(z, y, 1 - c)
    y_peer = index(z, 1 - y, c)
    z_peer = {d: index(along(d), y, c) for d in range(1, depth)}

    def local(src, dst, sem):
        copy = pltpu.make_async_copy(src, dst, sem)
        copy.start()
        return copy

    own_dx = local(dx_ref, dall.at[0, 0, 0], x_sem.at[0])
    first = tokens - half
    x_in = [
        local(px_ref.at[pl.ds(0, half)], xs.at[0], x_sem.at[1]),
        local(px_ref.at[pl.ds(half, first)], xs.at[1, pl.ds(0, first)], x_sem.at[2]),
        local(dx_ref, xs.at[1, pl.ds(first, decodes)], x_sem.at[3]),
    ]
    wk_in = {}
    for d in order:
        for yy in range(2):
            col = pl.multiple_of((along(d) * 2 + lax.rem(y + yy, 2)) * width, width)
            wk_in[d, yy] = local(wkv_ref.at[:, pl.ds(col, width)], wk.at[d, yy], wk_sem.at[d, yy])

    barrier = pltpu.get_barrier_semaphore()
    peers = [core_peer, y_peer] + [z_peer[d] for d in range(1, depth)]
    for peer in peers:
        pl.semaphore_signal(barrier, inc=1, device_id={"tp": peer}, device_id_type=pl.DeviceIdType.MESH)
    pl.semaphore_wait(barrier, len(peers))

    sends = []

    def send(src, dst, sem, peer, at=None, recv_at=None):
        copy = pltpu.make_async_remote_copy(
            src_ref=src,
            dst_ref=dst,
            send_sem=sem.at[(0,) + at],
            recv_sem=sem.at[(1,) + (recv_at or at)],
            device_id={"tp": peer},
            device_id_type=pl.DeviceIdType.MESH,
        )
        copy.start()
        sends.append(copy)
        return copy

    own_dx.wait()
    g_z = [
        send(dall.at[0, 0, 0], dall.at[0, 0, depth - d], g_sem, z_peer[d], (d,), (d,)) for d in range(1, depth)
    ]

    for copy in x_in:
        copy.wait()
    a_copy = {}
    for d in order:
        for yy in range(2):
            wk_in[d, yy].wait()
            part = jnp.dot(xs[1 - c], wk[d, yy], preferred_element_type=jnp.float32)
            a_send[d, yy] = part.astype(jnp.bfloat16)
        a_copy[d] = send(a_send.at[d], a_recv.at[d], a_sem, core_peer, (d,))

    wq_in = []
    for cc in range(2):
        for yy in range(2):
            for d in range(depth):
                row = pl.multiple_of(index(along(d), lax.rem(y + yy, 2), lax.rem(c + cc, 2)) * feats, feats)
                wq_in.append(local(wq_ref.at[pl.ds(row, feats)], wq.at[cc, yy, d], wq_sem.at[cc, yy, d]))
    b_copy = {}
    for d in order:
        for yy in range(2):
            a_own[d, yy] = jnp.dot(xs[c], wk[d, yy], preferred_element_type=jnp.float32)
        a_copy[d].wait_recv()
        b_send[d] = (a_own[d, 1] + a_recv[d, 1].astype(jnp.float32)).astype(jnp.bfloat16)
        b_copy[d] = send(b_send.at[d], b_recv.at[d], b_sem, y_peer, (d,))
        if d == order[0]:
            for copy in g_z:
                copy.wait_recv()
            g_y = send(dall.at[0, 0], dall.at[0, 1], g_sem, y_peer, (0,))
    wo_in = {}
    for d in order:
        for cc in (1, 0):
            for yy in (1, 0):
                col = pl.multiple_of(index(along(d), lax.rem(y + yy, 2), lax.rem(c + cc, 2)) * outw, outw)
                wo_in[d, yy, cc] = local(wo_ref.at[:, pl.ds(col, outw)], wo.at[d, yy, cc], wo_sem.at[d, yy, cc])

    c_copy = {}
    mine = None
    for d in order:
        b_copy[d].wait_recv()
        total = a_own[d, 0] + a_recv[d, 0].astype(jnp.float32) + b_recv[d].astype(jnp.float32)
        if d:
            c_send[d - 1] = total.astype(jnp.bfloat16)
            c_copy[d] = send(c_send.at[d - 1], c_recv.at[d - 1], c_sem, z_peer[d], (d - 1,))
        else:
            a_own[0, 0] = total
        if d == order[0]:
            g_y.wait_recv()
            g_c = send(dall.at[0], dall.at[1], g_sem, core_peer, (depth,))

    g_c.wait_recv()
    for copy in wq_in:
        copy.wait()
    q = jnp.zeros((decodes, wq.shape[-1]), jnp.float32)
    for cc in range(2):
        for yy in range(2):
            for d in range(depth):
                q = q + jnp.dot(dall[cc, yy, d], wq[cc, yy, d], preferred_element_type=jnp.float32)
    q = q.astype(jnp.bfloat16)
    heads = q.shape[1] // HD
    q = jnp.concatenate([q[:, h * HD : (h + 1) * HD] for h in range(heads)], axis=0)

    everything = 2 * half
    tok = lax.broadcasted_iota(jnp.int32, (1, everything), 1)
    fresh = tok - tokens
    tok_row = jnp.where(fresh >= 0, lax.rem(jnp.maximum(fresh, 0), rows), 0)
    tok_step = jnp.where(fresh >= 0, jnp.maximum(fresh, 0) // rows, -1)
    start = 0
    for i in range(pb_ref.shape[0]):
        end = start + pb_ref[i] * BLK
        tok_row = jnp.where((tok >= start) & (tok < end), pr_ref[i], tok_row)
        start = end
    which = lax.rem(lax.broadcasted_iota(jnp.int32, (heads * decodes, 1), 0), decodes)
    q_row, q_step = lax.rem(which, rows), which // rows
    visible = (tok_row == q_row) & (tok_step <= q_step)

    for d in range(1, depth):
        c_copy[d].wait_recv()
    total = a_own[0, 0]
    for d in range(1, depth):
        total = total + c_recv[d - 1].astype(jnp.float32)
    blocks = half // BLK
    blocked = total.reshape(blocks, BLK, width)
    top = jnp.max(jnp.abs(blocked), axis=1, keepdims=True)
    dequantized = []
    for e in range(2):
        part = blocked[:, :, e * HD : (e + 1) * HD]
        scale = jnp.max(top[:, :, e * HD : (e + 1) * HD], axis=2, keepdims=True) + 1e-06
        scale = scale.astype(jnp.bfloat16).astype(jnp.float32)
        stored = (part / scale).astype(jnp.bfloat16).astype(jnp.float32)
        dequantized.append(stored * scale)
    cached = jnp.concatenate(dequantized, axis=2).reshape(half, width)
    row = lax.broadcasted_iota(jnp.int32, (half, 1), 0) + c * half
    kv[c] = jnp.where(row < tokens, cached, total).astype(jnp.bfloat16)
    send(kv.at[c], kv.at[c], kv_sem, core_peer, (0,)).wait_recv()

    both = kv[...].reshape(everything, width)
    score = lax.dot_general(
        q, both[:, :HD], (((1,), (1,)), ((), ())), preferred_element_type=jnp.float32
    ) * (1.0 / math.sqrt(HD))
    score = jnp.where(visible, score, -jnp.inf)
    weight = jnp.exp(score - jnp.max(score, axis=1, keepdims=True))
    denominator = jnp.sum(weight, axis=1, keepdims=True)
    att = jnp.dot(weight.astype(jnp.bfloat16), both[:, HD:], preferred_element_type=jnp.float32)
    att = (att / denominator).astype(jnp.bfloat16)
    att = jnp.concatenate([att[h * decodes : (h + 1) * decodes] for h in range(heads)], axis=1)

    oa_copy, ob_copy, oc_copy = {}, {}, {}
    for d in order:
        for yy in (1, 0):
            wo_in[d, yy, 1].wait()
            oa_send[d, yy] = jnp.dot(att, wo[d, yy, 1], preferred_element_type=jnp.float32).astype(jnp.bfloat16)
        oa_copy[d] = send(oa_send.at[d], oa_recv.at[d], oa_sem, core_peer, (d,))
    for d in order:
        for yy in (1, 0):
            wo_in[d, yy, 0].wait()
            oa_own[d, yy] = jnp.dot(att, wo[d, yy, 0], preferred_element_type=jnp.float32)
        oa_copy[d].wait_recv()
        ob_send[d] = (oa_own[d, 1] + oa_recv[d, 1].astype(jnp.float32)).astype(jnp.bfloat16)
        ob_copy[d] = send(ob_send.at[d], ob_recv.at[d], ob_sem, y_peer, (d,))
    for d in order:
        ob_copy[d].wait_recv()
        total = oa_own[d, 0] + oa_recv[d, 0].astype(jnp.float32) + ob_recv[d].astype(jnp.float32)
        if d:
            oc_send[d - 1] = total.astype(jnp.bfloat16)
            oc_copy[d] = send(oc_send.at[d - 1], oc_recv.at[d - 1], oc_sem, z_peer[d], (d - 1,))
    for d in range(1, depth):
        oc_copy[d].wait_recv()
        total = total + oc_recv[d - 1].astype(jnp.float32)
    out_ref[...] = total.astype(out_ref.dtype)
    for copy in sends:
        copy.wait_send()


def fused_on_device(prompt_x, decode_x, w_query, w_keyval, w_out, prompt_blocks, prompt_row):
    depth = lax.axis_size("tp") // 4
    tokens, feats = prompt_x.shape
    steps, rows, _ = decode_x.shape
    decodes = steps * rows
    half = (tokens + decodes) // 2
    width = 2 * HD
    qw = w_query.shape[1]
    outw = w_out.shape[1] // (4 * depth)
    bf, f32 = jnp.bfloat16, jnp.float32
    vm, dma = pltpu.VMEM, pltpu.SemaphoreType.DMA
    anywhere = pl.BlockSpec(memory_space=pl.ANY)
    scalars = pl.BlockSpec(memory_space=pltpu.SMEM)
    out = pl.pallas_call(
        functools.partial(fused, depth, rows),
        out_shape=jax.ShapeDtypeStruct((decodes, outw), bf),
        in_specs=[scalars] * 2 + [anywhere] * 5,
        out_specs=pl.BlockSpec(memory_space=pltpu.VMEM),
        scratch_shapes=[
            vm((2, half, feats), bf),
            vm((depth, 2, feats, width), bf),
            vm((2, 2, depth, feats, qw), bf),
            vm((depth, 2, 2, w_out.shape[0], outw), bf),
            vm((2, 2, depth, decodes, feats), bf),
            vm((depth, 2, half, width), bf),
            vm((depth, 2, half, width), bf),
            vm((depth, 2, half, width), f32),
            vm((depth, half, width), bf),
            vm((depth, half, width), bf),
            vm((depth - 1, half, width), bf),
            vm((depth - 1, half, width), bf),
            vm((2, half, width), bf),
            vm((depth, 2, decodes, outw), bf),
            vm((depth, 2, decodes, outw), bf),
            vm((depth, 2, decodes, outw), f32),
            vm((depth, decodes, outw), bf),
            vm((depth, decodes, outw), bf),
            vm((depth - 1, decodes, outw), bf),
            vm((depth - 1, decodes, outw), bf),
            dma((4,)),
            dma((depth, 2)),
            dma((2, 2, depth)),
            dma((depth, 2, 2)),
            dma((2, depth + 1)),
            dma((2, depth)),
            dma((2, depth)),
            dma((2, depth - 1)),
            dma((2, 1)),
            dma((2, depth)),
            dma((2, depth)),
            dma((2, depth - 1)),
        ],
        compiler_params=pltpu.CompilerParams(
            collective_id=0, has_side_effects=True, vmem_limit_bytes=56 * 2**20
        ),
    )(prompt_blocks, prompt_row, prompt_x, decode_x.reshape(decodes, feats), w_keyval, w_query, w_out)
    return out.reshape(steps, rows, outw)


def solution(mesh):
    chip_per_head = mesh.shape["pool"] == 1 and mesh.shape["tp"] == 2 * KVH
    placed = (
        P(("group", "pool"), "tp"),
        P(None, ("group", "pool"), "tp"),
        P(None, "tp"),
        P("tp", None),
        P("tp", None),
        P("group"),
        P("group"),
    )
    return jax.shard_map(
        fused_on_device if chip_per_head else on_device,
        mesh=mesh,
        in_specs=placed,
        out_specs=P(None, ("group", "pool"), "tp"),
        check_vma=False,
    )
```

```python
import functools
import math

import jax
import jax.numpy as jnp
import numpy as np
from jax import lax
from jax.experimental import pallas as pl
from jax.experimental.pallas import tpu as pltpu
from jax.sharding import PartitionSpec as P

KVH = 8
HD = 128
BLK = 16


def block_rows(prompt_blocks, prompt_row, total_blocks):
    order = jnp.arange(prompt_blocks.shape[0], dtype=jnp.int32)
    block_ends = jnp.sum(jnp.where(order[None, :] <= order[:, None], prompt_blocks[None, :], 0), axis=1)
    positions = jnp.arange(total_blocks, dtype=jnp.int32)
    owner_seq = jnp.sum((block_ends[None, :] <= positions[:, None]).astype(jnp.int32), axis=1)
    seq_match = owner_seq[:, None] == jnp.arange(prompt_row.shape[0], dtype=jnp.int32)[None, :]
    return jnp.sum(jnp.where(seq_match, prompt_row[None, :], 0), axis=1)


def attend(queries, cache_vals, cache_scale, slot_row, fresh_keyval, row_ids):
    head_dim = queries.shape[-1]
    inverse_root = 1.0 / math.sqrt(head_dim)
    query_f32 = queries.astype(jnp.float32)
    scale_f32 = cache_scale.astype(jnp.float32)
    cache_keys = cache_vals[:, :, :head_dim].astype(jnp.float32) * scale_f32[:, 0][:, None, None]
    cache_values = cache_vals[:, :, head_dim:].astype(jnp.float32) * scale_f32[:, 1][:, None, None]
    cache_score = jnp.einsum("srgd,nkd->srgnk", query_f32, cache_keys) * inverse_root
    visible = slot_row[None, :] == row_ids[:, None]
    cache_score = jnp.where(visible[None, :, None, :, None], cache_score, -jnp.inf)
    fresh_f32 = fresh_keyval.astype(jnp.float32)
    fresh_score = jnp.einsum("srgd,trd->srgt", query_f32, fresh_f32[:, :, :head_dim]) * inverse_root
    step_index = jnp.arange(queries.shape[0], dtype=jnp.int32)
    causal = step_index[:, None] >= step_index[None, :]
    fresh_score = jnp.where(causal[:, None, None, :], fresh_score, -jnp.inf)
    top_score = jnp.maximum(jnp.max(cache_score, axis=(3, 4)), jnp.max(fresh_score, axis=3))
    cache_weight = jnp.exp(cache_score - top_score[..., None, None])
    fresh_weight = jnp.exp(fresh_score - top_score[..., None])
    denominator = jnp.sum(cache_weight, axis=(3, 4)) + jnp.sum(fresh_weight, axis=3)
    weighted = jnp.einsum("srgnk,nkd->srgd", cache_weight, cache_values)
    weighted = weighted + jnp.einsum("srgt,trd->srgd", fresh_weight, fresh_f32[:, :, head_dim:])
    return weighted / denominator[..., None]


def on_device(prompt_x, decode_x, w_query, w_keyval, w_out, prompt_blocks, prompt_row):
    tp_count = lax.axis_size("tp")
    pool_count = lax.axis_size("pool")
    tp_index = lax.axis_index("tp")
    pool_index = lax.axis_index("pool")
    half_tokens = prompt_x.shape[0]
    tokens_here = half_tokens // tp_count
    blocks_here = tokens_here // BLK
    half_blocks = half_tokens // BLK
    total_blocks = half_blocks * pool_count
    keyval = lax.psum_scatter(
        jnp.dot(prompt_x, w_keyval, preferred_element_type=jnp.float32),
        "tp",
        scatter_dimension=0,
        tiled=True,
    )
    blocked = keyval.reshape(blocks_here, BLK, KVH, 2, HD)
    scales = (jnp.max(jnp.abs(blocked), axis=(1, 4)) + 1e-06).astype(jnp.bfloat16)
    stored = (blocked / scales.astype(jnp.float32)[:, None, :, :, None]).astype(jnp.bfloat16)
    stored = stored.reshape(blocks_here, BLK, KVH, 2 * HD)
    slot_row_all = block_rows(prompt_blocks, prompt_row, total_blocks)
    row_half = decode_x.shape[1]
    owner_half = slot_row_all // row_half
    first_block = pool_index * half_blocks + tp_index * blocks_here
    mine_owner = lax.dynamic_slice_in_dim(owner_half, first_block, blocks_here, 0)
    dest_head = np.arange(tp_count) * KVH // tp_count
    by_head = jnp.stack([stored[:, :, int(h)] for h in dest_head])
    scale_head = jnp.stack([scales[:, int(h)] for h in dest_head])
    to_half = mine_owner[None, :] == jnp.arange(pool_count, dtype=jnp.int32)[:, None]
    zero_value = jnp.zeros((), jnp.bfloat16)
    send_vals = jnp.where(to_half[None, :, :, None, None], by_head[:, None], zero_value)
    send_scale = jnp.where(to_half[None, :, :, None], scale_head[:, None], zero_value)
    got_vals, got_scale = (
        lax.all_to_all(
            lax.all_to_all(send_vals, "tp", split_axis=0, concat_axis=0, tiled=True),
            "pool",
            split_axis=1,
            concat_axis=1,
            tiled=True,
        ),
        lax.all_to_all(
            lax.all_to_all(send_scale, "tp", split_axis=0, concat_axis=0, tiled=True),
            "pool",
            split_axis=1,
            concat_axis=1,
            tiled=True,
        ),
    )
    got_vals = got_vals.reshape(total_blocks, BLK, 2 * HD)
    got_scale = got_scale.reshape(total_blocks, 2)
    slot_row = (
        slot_row_all.reshape(pool_count, tp_count, blocks_here)
        .transpose(1, 0, 2)
        .reshape(total_blocks)
    )
    gathered = lax.all_gather(decode_x, "tp", axis=2, tiled=True)
    step_count, row_count, model_width = gathered.shape
    heads_here = w_query.shape[1] // HD
    queries = jnp.einsum("srd,de->sre", gathered, w_query, preferred_element_type=jnp.float32)
    queries = queries.astype(jnp.bfloat16).reshape(step_count, row_count, heads_here, HD)
    partial_new = jnp.einsum("srd,de->sre", decode_x, w_keyval, preferred_element_type=jnp.float32)
    summed_new = lax.psum(partial_new, "tp")
    fresh_keyval = summed_new.astype(jnp.bfloat16).reshape(step_count, row_count, KVH, 2 * HD)
    my_head = tp_index * KVH // tp_count
    fresh_keyval = lax.dynamic_index_in_dim(fresh_keyval, my_head, 2, keepdims=False)
    row_ids = pool_index * row_count + jnp.arange(row_count, dtype=jnp.int32)
    weighted = attend(queries, got_vals, got_scale, slot_row, fresh_keyval, row_ids)
    attended = weighted.reshape(step_count, row_count, heads_here * HD).astype(jnp.bfloat16)
    out_term = jnp.einsum("sre,ed->srd", attended, w_out, preferred_element_type=jnp.float32)
    return lax.psum_scatter(out_term, "tp", scatter_dimension=2, tiled=True).astype(jnp.bfloat16)


def fused(
    rows,
    pb_ref, pr_ref, px_ref, dx_ref, wkv_ref, wq_ref, wo_ref,
    out_ref,
    xs, wk, wq, wo, dall,
    a_send, a_recv, a_own,
    b_send, b_recv,
    c_send, c_recv,
    kv,
    oa_send, oa_recv,
    ob_send, ob_recv,
    oc_send, oc_recv, o_own, hidden, q_all, att_all,
    x_sem, wk_sem, wq_sem, wo_sem,
    g_sem, a_sem, b_sem, c_sem, kv_sem, oa_sem, ob_sem, oc_sem,
):
    me = lax.axis_index("tp")
    hi, lo, y, c = me // 8, lax.rem(me // 4, 2), lax.rem(me // 2, 2), lax.rem(me, 2)
    tokens, decodes = px_ref.shape[0], dx_ref.shape[0]
    feats = px_ref.shape[1]
    half = xs.shape[1]
    width = 2 * HD
    outw = out_ref.shape[1]
    order = (3, 2, 1, 0)

    def place(s, yy, cc):
        zz = lax.rem(hi + s // 2, 2) * 2 + lax.rem(lo + s % 2, 2)
        return (zz * 2 + lax.rem(y + yy, 2)) * 2 + lax.rem(c + cc, 2)

    core_peer, y_peer = place(0, 0, 1), place(0, 1, 0)
    lo_peer, hi_peer = place(1, 0, 0), place(2, 0, 0)
    z_peer = {3: lo_peer, 2: hi_peer, 1: lo_peer}

    def local(src, dst, sem):
        copy = pltpu.make_async_copy(src, dst, sem)
        copy.start()
        return copy

    own_dx = local(dx_ref, dall.at[0, 0, 0, 0], x_sem.at[0])
    first = tokens - half
    x_in = [
        local(px_ref.at[pl.ds(0, half)], xs.at[0], x_sem.at[1]),
        local(px_ref.at[pl.ds(half, first)], xs.at[1, pl.ds(0, first)], x_sem.at[2]),
        local(dx_ref, xs.at[1, pl.ds(first, decodes)], x_sem.at[3]),
    ]
    wk_in = {}
    for yy in (1, 0):
        for s in order:
            col = pl.multiple_of(place(s, yy, 0) // 2 * width, width)
            wk_in[s, yy] = local(wkv_ref.at[:, pl.ds(col, width)], wk.at[s, yy], wk_sem.at[s, yy])

    barrier = pltpu.get_barrier_semaphore()
    peers = [core_peer, y_peer, lo_peer, hi_peer]
    for peer in peers:
        pl.semaphore_signal(barrier, inc=1, device_id={"tp": peer}, device_id_type=pl.DeviceIdType.MESH)
    pl.semaphore_wait(barrier, len(peers))

    sends = []

    def remote(src, dst, sem, peer, at):
        return pltpu.make_async_remote_copy(
            src_ref=src,
            dst_ref=dst,
            send_sem=sem.at[(0,) + at],
            recv_sem=sem.at[(1,) + at],
            device_id={"tp": peer},
            device_id_type=pl.DeviceIdType.MESH,
        )

    def send(src, dst, sem, peer, at):
        copy = remote(src, dst, sem, peer, at)
        copy.start()
        sends.append(copy)
        return copy

    def loop(count, body):
        lax.fori_loop(0, count, lambda i, carry: (body(i), carry)[1], 0)

    piece = half // 2

    def by_rows(r, body):
        loop(piece // BLK, lambda i: body(pl.ds(pl.multiple_of(r * piece + i * BLK, BLK), BLK)))

    own_dx.wait()
    g_y = send(dall.at[0, 0, 0, 0], dall.at[0, 0, 0, 1], g_sem, y_peer, (0,))

    for copy in x_in:
        copy.wait()
    for copy in wk_in.values():
        copy.wait()

    def a_copy(s, yy):
        return remote(a_send.at[s, yy], a_recv.at[s, yy], a_sem, core_peer, (s, yy))

    def b_copy(s, r):
        at = pl.ds(r * piece, piece)
        return remote(b_send.at[s, at], b_recv.at[s, at], b_sem, y_peer, (s, r))

    def other_rows(s, yy):
        part = jnp.dot(xs[1 - c], wk[s, yy], preferred_element_type=jnp.float32)
        a_send[s, yy] = part.astype(jnp.bfloat16)
        a_copy(s, yy).start()

    def over_y(s):
        part = jnp.dot(xs[c], wk[s, 1], preferred_element_type=jnp.float32)
        a_copy(s, 1).wait_recv()
        b_send[s] = (part + a_recv[s, 1].astype(jnp.float32)).astype(jnp.bfloat16)

    def over_y_first(s):
        over_y(s)
        b_copy(s, 0).start()

    def stay(s):
        other_rows(s, 0)
        a_own[s] = jnp.dot(xs[c], wk[s, 0], preferred_element_type=jnp.float32)

    loop(4, lambda i: other_rows(3 - i, 1))
    g_y.wait_recv()
    g_hi = send(dall.at[0, 0, 0], dall.at[0, 0, 1], g_sem, hi_peer, (1,))
    loop(2, lambda i: over_y_first(3 - i))
    loop(2, lambda i: over_y(1 - i))
    wq_in = []
    for cc in range(2):
        for s in range(4):
            for yy in range(2):
                row = pl.multiple_of(place(s, yy, cc) * feats, feats)
                at = (cc, s % 2, s // 2, yy)
                wq_in.append(local(wq_ref.at[pl.ds(row, feats)], wq.at[at], wq_sem.at[at]))
    loop(4, lambda i: stay(3 - i))
    g_hi.wait_recv()
    g_lo = send(dall.at[0, 0], dall.at[0, 1], g_sem, lo_peer, (2,))
    wo_in = {}
    for yy in (1, 0):
        for s in order:
            for cc in (1, 0):
                col = pl.multiple_of(place(s, yy, cc) * outw, outw)
                wo_in[s, yy, cc] = local(wo_ref.at[:, pl.ds(col, outw)], wo.at[s, yy, cc], wo_sem.at[s, yy, cc])

    queue = [(3, 0), (2, 0), (3, 1), (2, 1), (1, 0), (1, 1), (0, 0), (0, 1)]
    begun = queue[:2]

    def begin(upto):
        for s, r in queue[len(begun) : upto]:
            b_copy(s, r).start()
            begun.append((s, r))

    def sum_y(k):
        s, r = queue[k]
        if r == 0:
            a_copy(s, 0).wait_recv()
        b_copy(s, r).wait_recv()
        begin(k + 4)
        if s == 2:
            c_copy[3, r].wait_recv()

        def rows_of(at):
            total = a_own[s, at] + a_recv[s, 0, at].astype(jnp.float32) + b_recv[s, at].astype(jnp.float32)
            if s == 2:
                total = total + c_recv[2, at].astype(jnp.float32)
            if s:
                c_send[s - 1, at] = total.astype(jnp.bfloat16)
            else:
                a_own[s, at] = total

        by_rows(r, rows_of)
        if s:
            at = pl.ds(r * piece, piece)
            c_copy[s, r] = send(c_send.at[s - 1, at], c_recv.at[s - 1, at], c_sem, z_peer[s], (s - 1, r))

    c_copy = {}
    sum_y(0)

    everything = 2 * half
    tok = lax.broadcasted_iota(jnp.int32, (1, everything), 1)
    fresh = tok - tokens
    tok_row = jnp.where(fresh >= 0, lax.rem(jnp.maximum(fresh, 0), rows), 0)
    tok_step = jnp.where(fresh >= 0, jnp.maximum(fresh, 0) // rows, -1)
    start = 0
    for i in range(pb_ref.shape[0]):
        end = start + pb_ref[i] * BLK
        tok_row = jnp.where((tok >= start) & (tok < end), pr_ref[i], tok_row)
        start = end
    which = lax.broadcasted_iota(jnp.int32, (decodes, 1), 0)
    q_row, q_step = lax.rem(which, rows), which // rows
    visible = (tok_row == q_row) & (tok_step <= q_step)
    hidden[...] = jnp.where(visible, 0.0, -jnp.inf)

    for k in (1, 2, 3):
        sum_y(k)
    g_lo.wait_recv()
    g_c = send(dall.at[0], dall.at[1], g_sem, core_peer, (3,))
    sum_y(4)

    g_c.wait_recv()
    for copy in wq_in:
        copy.wait()

    def project(i, q):
        at = (i // 8, i // 4 % 2, i // 2 % 2, i % 2)
        return q + jnp.dot(dall[at], wq[at], preferred_element_type=jnp.float32)

    q = lax.fori_loop(0, 16, project, jnp.zeros((decodes, wq.shape[-1]), jnp.float32)).astype(jnp.bfloat16)
    heads = q.shape[1] // HD
    for h in range(heads):
        q_all[h] = q[:, h * HD : (h + 1) * HD]
    sum_y(5)


    def store_rows(at):
        total = a_own[0, at] + c_recv[0, at].astype(jnp.float32) + c_recv[1, at].astype(jnp.float32)
        blocked = total.reshape(1, BLK, width)
        top = jnp.max(jnp.abs(blocked), axis=1, keepdims=True)
        dequantized = []
        for e in range(2):
            part = blocked[:, :, e * HD : (e + 1) * HD]
            scale = jnp.max(top[:, :, e * HD : (e + 1) * HD], axis=2, keepdims=True) + 1e-06
            scale = scale.astype(jnp.bfloat16).astype(jnp.float32)
            stored = (part / scale).astype(jnp.bfloat16).astype(jnp.float32)
            dequantized.append(stored * scale)
        cached = jnp.concatenate(dequantized, axis=2).reshape(BLK, width)
        row = lax.broadcasted_iota(jnp.int32, (BLK, 1), 0) + at.start + c * half
        kv[c, at] = jnp.where(row < tokens, cached, total).astype(jnp.bfloat16)

    kv_copy = []
    for r in range(2):
        sum_y(6 + r)
        c_copy[2, r].wait_recv()
        c_copy[1, r].wait_recv()
        by_rows(r, store_rows)
        at = pl.ds(r * piece, piece)
        kv_copy.append(send(kv.at[c, at], kv.at[c, at], kv_sem, core_peer, (r,)))
    for copy in kv_copy:
        copy.wait_recv()

    def attend_head(h):
        both = kv[...].reshape(everything, width)
        score = lax.dot_general(
            q_all[h], both[:, :HD], (((1,), (1,)), ((), ())), preferred_element_type=jnp.float32
        )
        score = score * (1.0 / math.sqrt(HD)) + hidden[...]
        weight = jnp.exp(score - jnp.max(score, axis=1, keepdims=True))
        denominator = jnp.sum(weight, axis=1, keepdims=True)
        att = jnp.dot(weight.astype(jnp.bfloat16), both[:, HD:], preferred_element_type=jnp.float32)
        att_all[h] = (att / denominator).astype(jnp.bfloat16)

    loop(heads, attend_head)
    for copy in wo_in.values():
        copy.wait()

    def oa_copy(s, yy):
        return remote(oa_send.at[s, yy], oa_recv.at[s, yy], oa_sem, core_peer, (s, yy))

    def ob_copy(s):
        return remote(ob_send.at[s], ob_recv.at[s], ob_sem, y_peer, (s,))

    def out_part(s, yy, cc):
        att = jnp.concatenate([att_all[h] for h in range(heads)], axis=1)
        return jnp.dot(att, wo[s, yy, cc], preferred_element_type=jnp.float32)

    def other_part(s, yy):
        oa_send[s, yy] = out_part(s, yy, 1).astype(jnp.bfloat16)
        oa_copy(s, yy).start()

    def out_over_y(s):
        part = out_part(s, 1, 0)
        oa_copy(s, 1).wait_recv()
        ob_send[s] = (part + oa_recv[s, 1].astype(jnp.float32)).astype(jnp.bfloat16)
        ob_copy(s).start()

    def out_stay(s):
        other_part(s, 0)
        o_own[s] = out_part(s, 0, 0)

    loop(4, lambda i: other_part(3 - i, 1))
    loop(4, lambda i: out_over_y(3 - i))
    loop(4, lambda i: out_stay(3 - i))
    oc_copy = {}
    for s in order:
        oa_copy(s, 0).wait_recv()
        ob_copy(s).wait_recv()
        total = o_own[s] + oa_recv[s, 0].astype(jnp.float32) + ob_recv[s].astype(jnp.float32)
        if s == 2:
            oc_copy[3].wait_recv()
            total = total + oc_recv[2].astype(jnp.float32)
        if s:
            oc_send[s - 1] = total.astype(jnp.bfloat16)
            oc_copy[s] = send(oc_send.at[s - 1], oc_recv.at[s - 1], oc_sem, z_peer[s], (s - 1,))
    for s in (1, 2):
        oc_copy[s].wait_recv()
        total = total + oc_recv[s - 1].astype(jnp.float32)
    out_ref[...] = total.astype(out_ref.dtype)
    for s in order:
        for yy in range(2):
            a_copy(s, yy).wait_send()
            oa_copy(s, yy).wait_send()
        b_copy(s, 0).wait_send()
        b_copy(s, 1).wait_send()
        ob_copy(s).wait_send()
    for copy in sends:
        copy.wait_send()


def fused_on_device(prompt_x, decode_x, w_query, w_keyval, w_out, prompt_blocks, prompt_row):
    depth = lax.axis_size("tp") // 4
    tokens, feats = prompt_x.shape
    steps, rows, _ = decode_x.shape
    decodes = steps * rows
    half = (tokens + decodes) // 2
    width = 2 * HD
    qw = w_query.shape[1]
    outw = w_out.shape[1] // (4 * depth)
    bf, f32 = jnp.bfloat16, jnp.float32
    vm, dma = pltpu.VMEM, pltpu.SemaphoreType.DMA
    anywhere = pl.BlockSpec(memory_space=pl.ANY)
    scalars = pl.BlockSpec(memory_space=pltpu.SMEM)
    out = pl.pallas_call(
        functools.partial(fused, rows),
        out_shape=jax.ShapeDtypeStruct((decodes, outw), bf),
        in_specs=[scalars] * 2 + [anywhere] * 5,
        out_specs=pl.BlockSpec(memory_space=pltpu.VMEM),
        scratch_shapes=[
            vm((2, half, feats), bf),
            vm((depth, 2, feats, width), bf),
            vm((2, 2, 2, 2, feats, qw), bf),
            vm((depth, 2, 2, w_out.shape[0], outw), bf),
            vm((2, 2, 2, 2, decodes, feats), bf),
            vm((depth, 2, half, width), bf),
            vm((depth, 2, half, width), bf),
            vm((depth, half, width), f32),
            vm((depth, half, width), bf),
            vm((depth, half, width), bf),
            vm((depth - 1, half, width), bf),
            vm((depth - 1, half, width), bf),
            vm((2, half, width), bf),
            vm((depth, 2, decodes, outw), bf),
            vm((depth, 2, decodes, outw), bf),
            vm((depth, decodes, outw), bf),
            vm((depth, decodes, outw), bf),
            vm((depth - 1, decodes, outw), bf),
            vm((depth - 1, decodes, outw), bf),
            vm((depth, decodes, outw), f32),
            vm((decodes, 2 * half), f32),
            vm((qw // HD, decodes, HD), bf),
            vm((qw // HD, decodes, HD), bf),
            dma((4,)),
            dma((depth, 2)),
            dma((2, 2, 2, 2)),
            dma((depth, 2, 2)),
            dma((2, 4)),
            dma((2, depth, 2)),
            dma((2, depth, 2)),
            dma((2, depth - 1, 2)),
            dma((2, 2)),
            dma((2, depth, 2)),
            dma((2, depth)),
            dma((2, depth - 1)),
        ],
        compiler_params=pltpu.CompilerParams(
            collective_id=0, has_side_effects=True, vmem_limit_bytes=56 * 2**20
        ),
    )(prompt_blocks, prompt_row, prompt_x, decode_x.reshape(decodes, feats), w_keyval, w_query, w_out)
    return out.reshape(steps, rows, outw)


def solution(mesh):
    chip_per_head = mesh.shape["pool"] == 1 and mesh.shape["tp"] == 2 * KVH
    placed = (
        P(("group", "pool"), "tp"),
        P(None, ("group", "pool"), "tp"),
        P(None, "tp"),
        P("tp", None),
        P("tp", None),
        P("group"),
        P("group"),
    )
    return jax.shard_map(
        fused_on_device if chip_per_head else on_device,
        mesh=mesh,
        in_specs=placed,
        out_specs=P(None, ("group", "pool"), "tp"),
        check_vma=False,
    )
```
